32 devices in a mesh: groups: 2 (over x), tensor: 16 (over z, y, core).
Axes of the slice: x: 2, y: 2, z: 4, core: 2. Of those that a mesh axis runs over, the one named last changes fastest.
Arguments:
- tokens: int32 [3, 32], P(None, 'groups'), parts along dimension 1, may hold values from 0 to 32767
- page_table: int32 [32, 2], P('groups'), parts along dimension 0, may hold values from 0 to 15, as said below
- embedding: bfloat16 [32768, 8192], P(None, 'tensor'), may hold values from -6 to 6
- norm_gain: float32 [8192], replicated, may hold values from 0.5 to 1.5
- x_weight: bfloat16 [8192, 16384], P(None, 'tensor'), may hold values from -0.0625 to 0.0625
- z_weight: bfloat16 [8192, 16384], P(None, 'tensor'), may hold values from -0.0625 to 0.0625
- conv_weight: float32 [4, 16384], P(None, 'tensor'), may hold values from -3 to 3
- conv_bias: float32 [16384], P('tensor'), may hold values from -3 to 3
- proj_weight: bfloat16 [16384, 544], P('tensor'), may hold values from -0.046875 to 0.046875
- delta_gain: float32 [512], replicated, may hold values from 0.5 to 1.5
- delta_weight: bfloat16 [512, 16384], P(None, 'tensor'), may hold values from -0.25 to 0.25
- delta_bias: float32 [16384], P('tensor'), may hold values from -5 to 0
- log_rates: float32 [16, 16384], P(None, 'tensor'), may hold values from -4 to 2.5
- skip_gain: float32 [16384], P('tensor'), may hold values from 0.5 to 2
- out_weight: bfloat16 [16384, 8192], P('tensor'), may hold values from -0.0625 to 0.0625
- ssm_pages: bfloat16 [32, 16, 16384], P(('groups', 'tensor')), parts along dimension 0, may hold values from -6 to 6
- conv_pages: bfloat16 [32, 3, 16384], P(('groups', 'tensor')), parts along dimension 0, may hold values from -6 to 6
Outputs:
- hidden_out: bfloat16 [3, 32, 8192], P(None, 'groups', 'tensor'), parts along dimension 1
- ssm_out: bfloat16 [32, 16, 16384], P(('groups', 'tensor')), parts along dimension 0
- conv_out: bfloat16 [32, 3, 16384], P(('groups', 'tensor')), parts along dimension 0
The draws below stay inside these ranges and needn't reach their ends.
There are 2 independent parts, one for each index of `groups`. The reference program is written for one: setup_inputs(seed, part) draws one part's arguments, and reference() takes and returns one part's arrays. A program takes and returns all parts, laid end to end along the dimension named above; an argument that names none is the same for every part. Nothing has to cross between parts.
Inputs may be any that keep to these rules, and one draw needn't show every extreme that they name: `page_table`: column 0 is an owner index below 16, column 1 a slot below 1; every pair of owner and slot is named by exactly one row.
All inputs are finite; a program needn't handle non-finite values.
Results may differ from the reference program's by a relative error of at most 0.0068.
Values may be sent and summed in bfloat16 or wider, within the bound.
A program may use at most 256 MiB of HBM per device.

```python
import math
import jax
import jax.numpy as jnp
import numpy as np
from jax import lax

D = 8192
D_INNER = 16384
N_STATE = 16
CONV = 4
RANK = 512
VOCAB = 32768
STEPS = 3
SLOTS = 1
ROWS = 16


def draw_page_table(key, part):
    key = jax.random.fold_in(key, 11)
    shuffled = jax.random.permutation(key, ROWS).astype(jnp.int32)
    return jnp.stack([shuffled // SLOTS, shuffled % SLOTS], axis=1).astype(jnp.int32)


def with_ends(result, own_key, smallest, high):
    dims = result.shape
    spot = [jax.random.randint(jax.random.fold_in(own_key, axis), (), 0, dims[axis]) for axis in range(len(dims))]
    result = result.at[tuple(spot)].set(smallest)
    longest = dims.index(max(dims))
    spot[longest] = (spot[longest] + 1) % dims[longest]
    return result.at[tuple(spot)].set(high)


def spiked(drawn, rng, source, target, blocks, factor):
    owner, partner = [(jnp.arange(drawn.shape[dim]) // (drawn.shape[dim] // blocks)).reshape([-1 if axis == dim else 1 for axis in range(drawn.ndim)]) for dim in (source, target)]
    chosen = jax.random.permutation(rng, blocks)[partner]
    strong = (owner == chosen) | (owner == (partner + blocks // 2) % blocks)
    return jnp.where(strong, factor * drawn, drawn)


def shard_levels(stream_key, dims, split, least, largest):
    def one(dim, blocks):
        draws = jax.random.uniform(jax.random.fold_in(jax.random.fold_in(stream_key, 6), dim), (blocks,), jnp.float32, least / len(split), largest / len(split))
        return jnp.repeat(jnp.exp(draws), dims[dim] // blocks).reshape((-1,) + (1,) * (len(dims) - dim - 1))

    factor_of = one(*split[0])
    for cut in split[1:]:
        factor_of = factor_of * one(*cut)
    return factor_of


def rank_bounds(number_of, slope):
    loads = [(1 << 20) // math.isqrt(rank ** slope) + 1 for rank in range(1, number_of + 1)]
    scale = 1 + sum(loads) // (1 << 30)
    return np.cumsum(np.array([max(1, weight // scale) for weight in loads]))


def ranked_ids(rng, dims, amount, skew):
    table = rank_bounds(amount, skew)
    pick = jax.random.randint(jax.random.fold_in(rng, 1), dims, 0, int(table[amount - 1]))
    standing = jnp.searchsorted(jnp.asarray(table, jnp.int32), pick, side="right")
    return jax.random.permutation(jax.random.fold_in(rng, 2), amount)[standing].astype(jnp.int32)


def noise(key, shape, deviation, reach, cuts=(), kind=jnp.bfloat16):
    array = jax.random.normal(key, shape, jnp.float32) * deviation
    if len(cuts) > 0:
        array = shard_levels(key, shape, cuts, -0.22, 0.18) * array
    return jnp.clip(array, min=-reach, max=reach).astype(kind)


def gaussian_with(own_key, shape, width, bound, split, heavy, held_as=jnp.bfloat16):
    drawn = width * jax.random.normal(own_key, shape, jnp.float32)
    if split:
        drawn = drawn * shard_levels(own_key, shape, split, -0.22, 0.18)
    return jnp.clip(spiked(drawn, jax.random.fold_in(own_key, 3), *heavy), -bound, bound).astype(held_as)


def setup_inputs(seed: int = 0, part: int = 0) -> dict:
    streams_of = jax.random.split(jax.random.key(seed), 18)
    part_splits = jax.random.split(jax.random.fold_in(streams_of[17], part), 18)
    return {
        "tokens": with_ends(ranked_ids(part_splits[0], (STEPS, ROWS), VOCAB, 2), jax.random.fold_in(part_splits[0], 3), 0, VOCAB - 1).astype(jnp.int32),
        "page_table": draw_page_table(jax.random.fold_in(jax.random.fold_in(streams_of[17], part), 71), part),
        "embedding": noise(streams_of[2], (VOCAB, D), 1.0, 6.0, ((1, 16),)),
        "norm_gain": jnp.clip(1.0 + 0.1 * jax.random.normal(streams_of[3], (D,), jnp.float32), 0.5, 1.5),
        "x_weight": noise(streams_of[4], (D, D_INNER), D ** -0.5, 0.0625, ((1, 16),)),
        "z_weight": noise(streams_of[5], (D, D_INNER), D ** -0.5, 0.0625, ((1, 16),)),
        "conv_weight": noise(streams_of[6], (CONV, D_INNER), 0.5, 3.0, ((1, 16),), jnp.float32),
        "conv_bias": noise(streams_of[7], (D_INNER,), 0.5, 3.0, ((0, 16),), jnp.float32),
        "proj_weight": noise(streams_of[8], (D_INNER, RANK + 2 * N_STATE), D_INNER ** -0.5, 0.046875, ((0, 16),)),
        "delta_gain": jnp.clip(1.0 + 0.1 * jax.random.normal(streams_of[9], (RANK,), jnp.float32), 0.5, 1.5),
        "delta_weight": noise(streams_of[10], (RANK, D_INNER), RANK ** -0.5, 0.25, ((1, 16),)),
        "delta_bias": jnp.clip(-5.0 + 5.0 * jax.random.uniform(streams_of[11], (D_INNER,), jnp.float32) ** shard_levels(streams_of[11], (D_INNER,), ((0, 16),), -0.2, 0.2), -5.0, 0.0),
        "log_rates": jnp.clip(-4.0 + 6.5 * jax.random.uniform(streams_of[12], (N_STATE, D_INNER), jnp.float32) ** shard_levels(streams_of[12], (N_STATE, D_INNER), ((1, 16),), -0.2, 0.2), -4.0, 2.5),
        "skip_gain": jnp.clip(0.5 + 1.5 * jax.random.uniform(streams_of[13], (D_INNER,), jnp.float32) ** shard_levels(streams_of[13], (D_INNER,), ((0, 16),), -0.2, 0.2), 0.5, 2.0),
        "out_weight": gaussian_with(streams_of[14], (D_INNER, D), D_INNER ** -0.5, 0.0625, ((0, 16),), (0, 1, 16, 2.0)),
        "ssm_pages": noise(part_splits[15], (ROWS, N_STATE, D_INNER), 1.0, 6.0, ((0, 16),)),
        "conv_pages": noise(part_splits[16], (ROWS, CONV - 1, D_INNER), 1.0, 6.0, ((0, 16),)),
    }


def reference(tokens, page_table, embedding, norm_gain, x_weight, z_weight, conv_weight, conv_bias, proj_weight, delta_gain, delta_weight, delta_bias, log_rates, skip_gain, out_weight, ssm_pages, conv_pages):
    page_index = (page_table[:, 0] * SLOTS + page_table[:, 1]).astype(jnp.int32)
    ssm_state = ssm_pages[page_index].astype(jnp.float32)
    window = conv_pages[page_index]
    rates = -jnp.exp(log_rates)
    outputs = []
    for position in range(STEPS):
        embedded = embedding[tokens[position]]
        values = embedded.astype(jnp.float32)
        normed = (values * lax.rsqrt(lax.optimization_barrier(jnp.mean(values * values, axis=-1, keepdims=True)) + 1e-06) * norm_gain).astype(jnp.bfloat16)
        x_inner = jnp.dot(normed, x_weight, preferred_element_type=jnp.float32).astype(jnp.bfloat16)
        z_inner = jnp.dot(normed, z_weight, preferred_element_type=jnp.float32)
        conv_input = jnp.concatenate([window, x_inner[:, None, :]], axis=1).astype(jnp.float32)
        conv_act = jax.nn.silu(lax.optimization_barrier(jnp.sum(conv_input * conv_weight[None], axis=1)) + conv_bias)
        conv_bf = conv_act.astype(jnp.bfloat16)
        projected = jnp.dot(conv_bf, proj_weight, preferred_element_type=jnp.float32)
        delta_low = projected[:, :RANK]
        input_mat = projected[:, RANK:RANK + N_STATE]
        output_mat = projected[:, RANK + N_STATE:]
        delta_norm = (delta_low * lax.rsqrt(lax.optimization_barrier(jnp.mean(delta_low * delta_low, axis=-1, keepdims=True)) + 1e-06) * delta_gain).astype(jnp.bfloat16)
        delta = jax.nn.softplus(jnp.dot(delta_norm, delta_weight, preferred_element_type=jnp.float32) + delta_bias)
        ssm_state = ssm_state * jnp.exp(delta[:, None, :] * rates[None]) + (delta * conv_act)[:, None, :] * input_mat[:, :, None]
        readout = (lax.optimization_barrier(jnp.sum(ssm_state * output_mat[:, :, None], axis=1)) + skip_gain * conv_act) * jax.nn.silu(z_inner)
        readout = readout.astype(jnp.bfloat16)
        mixer_out = jnp.dot(readout, out_weight, preferred_element_type=jnp.float32)
        outputs.append((values + mixer_out).astype(jnp.bfloat16))
        window = jnp.concatenate([window[:, 1:], x_inner[:, None, :]], axis=1)
    hidden_out = jnp.stack(outputs)
    ssm_out = jnp.zeros_like(ssm_pages).at[page_index].set(ssm_state.astype(jnp.bfloat16))
    conv_out = jnp.zeros_like(conv_pages).at[page_index].set(window)
    return (hidden_out, ssm_out, conv_out)
```

```python
import functools

import jax
import jax.numpy as jnp
from jax import lax
from jax.experimental import pallas as pl
from jax.experimental.pallas import tpu as pltpu
from jax.sharding import PartitionSpec as P

LANES = 128
F32 = jnp.float32
BF16 = jnp.bfloat16


def sigmoid(v):
    return 1.0 / (1.0 + jnp.exp(-v))


def kernel(
    n, steps, slots, rank, states,
    rows_ref, gain_ref, conv_w_ref, conv_b_ref, dgain_ref, dbias_ref, lograte_ref, skip_ref,
    xw_hbm, zw_hbm, proj_hbm, dw_hbm, ow_hbm, ssm_hbm, conv_hbm,
    hid_ref, ssm_out, conv_out,
    xw, zw, ow, pw, dw,
    gath, accx, accz, ssq, state_in, state_fin, conv_in, conv_fin, win, act, delta, ysum,
    pf, part, part_in, red_out, proj_all, proj_f, mats, gated,
    send_a, recv_a, send_b, recv_b, send_c, recv_c,
    xw_sem, zw_sem, ow_sem, misc_sem,
    g_recv, g_s1, g_s2, g_s3,
    st_recv, st_send, cv_recv, cv_send,
    p_recv, p_send, q_recv, q_send,
    a_recv, a_send, b_recv, b_send, c_recv, c_send,
    so_recv, so_send, co_recv, co_send,
):
    me = lax.axis_index("tensor")
    bits = n.bit_length() - 1

    def xor(a, b):
        if isinstance(a, int) and isinstance(b, int):
            return a ^ b
        out = 0
        for k in range(bits):
            out = out + ((a // (1 << k)) % 2 + (b // (1 << k)) % 2) % 2 * (1 << k)
        return out

    rows = rows_ref.shape[0]
    per = rows // steps
    dl = rows_ref.shape[1]
    cl = accx.shape[1]
    d_model = n * dl
    q = n // 4

    def order(i):
        return (i % (n // 2)) // 2 * 4 + i // (n // 2) * 2 + i % 2

    def out_order(i):
        return jnp.where(
            i < n // 2, 2 * i + 1,
            jnp.where(i < n // 2 + q, 4 * (i - n // 2) + 2, (4 * (i - n // 2 - q) + 4) % n),
        )

    def cols(owner, width):
        return pl.ds(pl.multiple_of(owner * width, width), width)

    def x_load(i):
        src = xw_hbm.at[cols(xor(me, order(i)), dl), :]
        return pltpu.make_async_copy(src, xw.at[i], xw_sem.at[i])

    def z_load(i):
        src = zw_hbm.at[cols(xor(me, order(i)), dl), :]
        return pltpu.make_async_copy(src, zw.at[i], zw_sem.at[i])

    def o_load(i):
        if dl % LANES == 0:
            src = ow_hbm.at[:, cols(xor(me, out_order(i)), dl)]
        else:
            src = ow_hbm.at[xor(me, out_order(i))]
        return pltpu.make_async_copy(src, ow.at[i], ow_sem.at[i])

    p_load = pltpu.make_async_copy(proj_hbm, pw, misc_sem.at[0])
    d_load = pltpu.make_async_copy(dw_hbm, dw, misc_sem.at[1])
    own_state = pltpu.make_async_copy(ssm_hbm.at[:, :, cols(me, cl)], state_in.at[me], misc_sem.at[2])
    own_conv = pltpu.make_async_copy(conv_hbm.at[:, :, cols(me, cl)], conv_in.at[me], misc_sem.at[3])

    def remote(src, dst, ssem, rsem, peer):
        return pltpu.make_async_remote_copy(
            src_ref=src, dst_ref=dst, send_sem=ssem, recv_sem=rsem,
            device_id={"tensor": peer}, device_id_type=pl.DeviceIdType.MESH,
        )

    def to_core(j):
        return remote(gath.at[j], gath.at[j + 1], g_s1.at[j // 2], g_recv.at[j + 1], xor(me, 1))

    def to_side(j):
        return remote(gath.at[j], gath.at[j + 2], g_s2.at[j // 4], g_recv.at[j + 2], xor(me, 2))

    def to_far(k):
        return remote(gath.at[0], gath.at[4 * k], g_s3.at[k], g_recv.at[4 * k], xor(me, 4 * k))

    def got(j):
        return remote(gath.at[0], gath.at[j], g_s3.at[0], g_recv.at[j], xor(me, 1)).wait_recv()

    def state_copy(j, at):
        return remote(ssm_hbm.at[:, :, cols(xor(me, j), cl)], state_in.at[at], st_send.at[j], st_recv.at[j], xor(me, j))

    def conv_copy(j, at):
        return remote(conv_hbm.at[:, :, cols(xor(me, j), cl)], conv_in.at[at], cv_send.at[j], cv_recv.at[j], xor(me, j))

    def loop(lo, hi):
        def wrap(f):
            lax.fori_loop(lo, hi, lambda i, c: (f(i), c)[1], 0)
        return wrap

    @loop(0, min(4, n))
    def _(i):
        x_load(i).start()
        z_load(i).start()

    barrier = pltpu.get_barrier_semaphore()

    @loop(1, n)
    def _(j):
        pl.semaphore_signal(barrier, inc=1, device_id={"tensor": xor(me, j)}, device_id_type=pl.DeviceIdType.MESH)

    gath[0] = rows_ref[...]

    @loop(min(4, n), n)
    def _(i):
        x_load(i).start()
        z_load(i).start()

    p_load.start()
    d_load.start()
    own_state.start()
    own_conv.start()
    pl.semaphore_wait(barrier, n - 1)

    @loop(1, q)
    def _(k):
        to_far(k).start()

    to_side(0).start()
    to_core(0).start()

    accx[...] = jnp.zeros_like(accx)
    accz[...] = jnp.zeros_like(accz)
    ssq[...] = jnp.zeros_like(ssq)
    pf[...] = jnp.zeros_like(pf)

    @loop(0, n)
    def _(i):
        @pl.when(i >= 1)
        def _():
            conv_copy(i, me).start()
            state_copy(i, me).start()

        @pl.when((i % 2 == 0) & (i + 2 < n))
        def _():
            j = order(i + 2)
            got(j)
            to_core(j).start()

            @pl.when(j % 4 == 0)
            def _():
                to_side(j).start()

        j = order(i)

        @pl.when(i % 2 == 1)
        def _():
            got(j)

        e = gath[j].astype(F32)
        ssq[...] += jnp.sum(e * e, axis=1, keepdims=True)
        a = (e * gain_ref[xor(me, j)]).astype(BF16)
        x_load(i).wait()
        accx[...] += jnp.dot(a, xw[i], preferred_element_type=F32)
        z_load(i).wait()
        accz[...] += jnp.dot(a, zw[i], preferred_element_type=F32)

    @loop(0, n)
    def _(i):
        o_load(i).start()

    own_conv.wait()

    @loop(1, n)
    def _(j):
        conv_copy(j, xor(me, j)).wait_recv()

    @loop(0, n)
    def _(r):
        for s in range(slots):
            w = conv_in[r, s].astype(F32)
            for k in range(w.shape[0]):
                win[pl.ds(k * per + r * slots + s, 1), :] = w[k : k + 1]

    scale = lax.rsqrt(ssq[...] / d_model + 1e-06)
    taps = conv_w_ref.shape[0]
    win[pl.ds((taps - 1) * per, rows), :] = (accx[...] * scale).astype(BF16).astype(F32)
    zv = accz[...] * scale
    accz[...] = zv * sigmoid(zv)
    for t in range(steps):
        pre = conv_b_ref[...]
        for k in range(taps):
            pre = pre + win[pl.ds((t + k) * per, per), :] * conv_w_ref[k : k + 1]
        act[pl.ds(t * per, per), :] = pre * sigmoid(pre)

    p_load.wait()
    width = proj_hbm.shape[1]
    pf[:, :width] = jnp.dot(act[...].astype(BF16), pw[...], preferred_element_type=F32)
    blocks = pf.shape[1] // LANES
    tiles = part.shape[1]
    used = rows // 16 * blocks
    for k in range(used, n * tiles):
        part[k // tiles, k % tiles] = jnp.zeros((16, LANES), BF16)
    for k in range(used):
        g, b = divmod(k, blocks)
        part[k // tiles, k % tiles] = pf[16 * g : 16 * g + 16, LANES * b : LANES * b + LANES].astype(BF16)

    def sum_copy(j):
        return remote(part.at[xor(me, j)], part_in.at[j], p_send.at[j], p_recv.at[j], xor(me, j))

    def share_copy(j, at):
        return remote(red_out, proj_all.at[at], q_send.at[j], q_recv.at[j], xor(me, j))

    @loop(1, n)
    def _(j):
        sum_copy(n - j).start()

    part_in[0] = part[me]

    @loop(1, n)
    def _(j):
        sum_copy(j).wait_recv()

    red = jnp.sum(part_in[...].astype(F32), axis=0).astype(BF16)
    red_out[...] = red
    proj_all[me] = red

    @loop(1, n)
    def _(j):
        share_copy(n - j, me).start()

    @loop(1, n)
    def _(j):
        share_copy(j, xor(me, j)).wait_recv()

    for k in range(used):
        g, b = divmod(k, blocks)
        proj_f[16 * g : 16 * g + 16, LANES * b : LANES * b + LANES] = proj_all[k // tiles, k % tiles].astype(F32)

    low = proj_f[:, :rank]
    mats[...] = proj_f[:, rank : rank + LANES]
    norm = (low * lax.rsqrt(jnp.mean(low * low, axis=1, keepdims=True) + 1e-06) * dgain_ref[...]).astype(BF16)
    d_load.wait()
    pre = jnp.dot(norm, dw[...], preferred_element_type=F32) + dbias_ref[...]
    delta[...] = jnp.maximum(pre, 0.0) + jnp.log1p(jnp.exp(-jnp.abs(pre)))

    own_state.wait()
    rates = -jnp.exp(lograte_ref[...])

    def state_back(j, at):
        return remote(state_fin.at[xor(me, j)], ssm_out.at[:, :, cols(at, cl)], so_send.at[j], so_recv.at[j], xor(me, j))

    def conv_back(j, at):
        return remote(conv_fin.at[xor(me, j)], conv_out.at[:, :, cols(at, cl)], co_send.at[j], co_recv.at[j], xor(me, j))

    own_state_back = pltpu.make_async_copy(state_fin.at[me], ssm_out.at[:, :, cols(me, cl)], misc_sem.at[2])
    own_conv_back = pltpu.make_async_copy(conv_fin.at[me], conv_out.at[:, :, cols(me, cl)], misc_sem.at[3])
    lane = lax.broadcasted_iota(jnp.int32, (2 * states, LANES), 1)
    diag = lane == lax.broadcasted_iota(jnp.int32, (2 * states, LANES), 0)

    @loop(0, n)
    def _(i):
        j = n - 1 - i
        owner = xor(me, j)

        @pl.when(j > 0)
        def _():
            state_copy(j, owner).wait_recv()

        for s in range(slots):
            r = owner * slots + s
            h = state_in[owner, s].astype(F32)
            kept = []
            for t in range(steps):
                at = pl.ds(t * per + r, 1)
                both = jnp.sum(jnp.where(diag, mats[at, :], 0.0), axis=1, keepdims=True)
                dt = delta[at, :]
                h = h * jnp.exp(dt * rates) + (dt * act[at, :]) * both[:states]
                ysum[at, :] = jnp.sum(h * both[states:], axis=0, keepdims=True)
            state_fin[owner, s] = h.astype(BF16)
            kept = [win[pl.ds((steps + k) * per + r, 1), :] for k in range(taps - 1)]
            conv_fin[owner, s] = jnp.concatenate(kept, axis=0).astype(BF16)

        @pl.when(j > 0)
        def _():
            state_back(j, me).start()
            conv_back(j, me).start()

    own_state_back.start()
    own_conv_back.start()
    gated[...] = ((ysum[...] + skip_ref[...] * act[...]) * accz[...]).astype(BF16)

    def a_copy(k):
        return remote(send_a.at[k], recv_a.at[k], a_send.at[k], a_recv.at[k], xor(me, 1))

    def b_copy(k):
        return remote(send_b.at[k], recv_b.at[k], b_send.at[k], b_recv.at[k], xor(me, 2))

    def c_copy(k):
        return remote(send_c.at[k], recv_c.at[k], c_send.at[k], c_recv.at[k], xor(me, 4 * k))

    def product(i):
        o_load(i).wait()
        return jnp.dot(gated[...], ow[i], preferred_element_type=F32)

    @loop(0, n // 2)
    def _(i):
        send_a[i] = product(i).astype(BF16)
        a_copy(i).start()

    @loop(0, q)
    def _(k):
        total = product(n // 2 + k)
        a_copy(2 * k + 1).wait_recv()
        send_b[k] = (total + recv_a[2 * k + 1].astype(F32)).astype(BF16)
        b_copy(k).start()

    @loop(1, q)
    def _(k):
        total = product(n // 2 + q + k - 1)
        a_copy(2 * k).wait_recv()
        b_copy(k).wait_recv()
        send_c[k] = (total + recv_a[2 * k].astype(F32) + recv_b[k].astype(F32)).astype(BF16)
        c_copy(k).start()

    total = product(n - 1) + rows_ref[...].astype(F32)
    a_copy(0).wait_recv()
    b_copy(0).wait_recv()
    accum = total + recv_a[0].astype(F32) + recv_b[0].astype(F32)
    recv_c[0] = jnp.zeros((rows, dl), BF16)

    @loop(1, q)
    def _(k):
        c_copy(k).wait_recv()

    hid_ref[...] = (accum + jnp.sum(recv_c[...].astype(F32), axis=0)).astype(BF16)

    own_state_back.wait()
    own_conv_back.wait()

    @loop(1, n)
    def _(j):
        state_back(j, xor(me, j)).wait_recv()
        conv_back(j, xor(me, j)).wait_recv()
        state_back(j, me).wait_send()
        conv_back(j, me).wait_send()
        state_copy(j, me).wait_send()
        conv_copy(j, me).wait_send()
        sum_copy(j).wait_send()
        share_copy(j, me).wait_send()

    @loop(1, q)
    def _(k):
        to_far(k).wait_send()
        c_copy(k).wait_send()

    @loop(0, q)
    def _(k):
        to_side(4 * k).wait_send()
        b_copy(k).wait_send()

    @loop(0, n // 2)
    def _(k):
        to_core(2 * k).wait_send()
        a_copy(k).wait_send()


def body(
    n, tokens, page_table, embedding, norm_gain, x_weight, z_weight, conv_weight, conv_bias, proj_weight,
    delta_gain, delta_weight, delta_bias, log_rates, skip_gain, out_weight, ssm_pages, conv_pages,
):
    steps, per = tokens.shape
    slots, states, _ = ssm_pages.shape
    window = conv_pages.shape[1]
    rank, cl = delta_weight.shape
    dl = embedding.shape[1]
    rows = steps * per
    q = n // 4
    page = page_table[:, 0] * slots + page_table[:, 1]
    hit = page[:, None] == jnp.arange(per, dtype=page.dtype)[None]
    paged = jnp.sum(jnp.where(hit[None], tokens[:, :, None], 0), axis=1)
    local_rows = embedding[paged.reshape(-1)]
    width = proj_weight.shape[1]
    blocks = -(-width // LANES)
    tiles = -(-(rows // 16 * blocks) // n)
    if dl % LANES == 0:
        out_w = out_weight
    else:
        out_w = out_weight.reshape(cl, n, dl).transpose(1, 0, 2)
    vm = pl.BlockSpec(memory_space=pltpu.VMEM)
    hbm = pl.BlockSpec(memory_space=pl.ANY)
    dma = pltpu.SemaphoreType.DMA
    V = pltpu.VMEM
    hid, ssm_out, conv_out = pl.pallas_call(
        functools.partial(kernel, n, steps, slots, rank, states),
        out_shape=(
            jax.ShapeDtypeStruct((rows, dl), BF16),
            jax.ShapeDtypeStruct(ssm_pages.shape, BF16),
            jax.ShapeDtypeStruct(conv_pages.shape, BF16),
        ),
        in_specs=[vm] * 8 + [hbm] * 7,
        out_specs=(vm, hbm, hbm),
        scratch_shapes=[
            V((n, dl, cl), BF16), V((n, dl, cl), BF16), V((n, cl, dl), BF16), V((cl, width), BF16), V((rank, cl), BF16),
            V((n, rows, dl), BF16), V((rows, cl), F32), V((rows, cl), F32), V((rows, 1), F32),
            V((n, slots, states, cl), BF16), V((n, slots, states, cl), BF16),
            V((n, slots, window, cl), BF16), V((n, slots, window, cl), BF16),
            V((window * per + rows, cl), F32), V((rows, cl), F32), V((rows, cl), F32), V((rows, cl), F32),
            V((rows, blocks * LANES), F32), V((n, tiles, 16, LANES), BF16), V((n, tiles, 16, LANES), BF16),
            V((tiles, 16, LANES), BF16), V((n, tiles, 16, LANES), BF16), V((rows, blocks * LANES), F32), V((rows, LANES), F32), V((rows, cl), BF16),
            V((n // 2, rows, dl), BF16), V((n // 2, rows, dl), BF16),
            V((q, rows, dl), BF16), V((q, rows, dl), BF16), V((q, rows, dl), BF16), V((q, rows, dl), BF16),
            dma((n,)), dma((n,)), dma((n,)), dma((4,)),
            dma((n,)), dma((n // 2,)), dma((q,)), dma((q,)),
        ] + [dma((n,))] * 8 + [
            dma((n // 2,)), dma((n // 2,)), dma((q,)), dma((q,)), dma((q,)), dma((q,)),
        ] + [dma((n,))] * 4,
        compiler_params=pltpu.CompilerParams(
            collective_id=0, has_side_effects=True, vmem_limit_bytes=62 * 1024 * 1024
        ),
        cost_estimate=pl.CostEstimate(flops=2 * rows * cl * dl * n * 3, bytes_accessed=6 * cl * dl * n, transcendentals=0),
    )(
        local_rows, norm_gain.reshape(n, 1, dl), conv_weight, conv_bias.reshape(1, cl), delta_gain.reshape(1, rank),
        delta_bias.reshape(1, cl), log_rates, skip_gain.reshape(1, cl),
        x_weight, z_weight, proj_weight, delta_weight, out_w, ssm_pages, conv_pages,
    )
    return hid.reshape(steps, per, dl)[:, page], ssm_out, conv_out


def solution(mesh):
    placed = (
        P(None, "groups"),
        P("groups", None),
        P(None, "tensor"),
        P(),
        P(None, "tensor"),
        P(None, "tensor"),
        P(None, "tensor"),
        P("tensor"),
        P("tensor", None),
        P(),
        P(None, "tensor"),
        P("tensor"),
        P(None, "tensor"),
        P("tensor"),
        P("tensor", None),
        P(("groups", "tensor"), None, None),
        P(("groups", "tensor"), None, None),
    )
    return jax.shard_map(
        functools.partial(body, mesh.shape["tensor"]),
        mesh=mesh,
        in_specs=placed,
        out_specs=(
            P(None, "groups", "tensor"),
            P(("groups", "tensor"), None, None),
            P(("groups", "tensor"), None, None),
        ),
        check_vma=False,
    )
```

```python
import functools

import jax
import jax.numpy as jnp
from jax import lax
from jax.experimental import pallas as pl
from jax.experimental.pallas import tpu as pltpu
from jax.sharding import PartitionSpec as P

LANES = 128
PIECES = 4
SUM_TYPE = jnp.float32
F32 = jnp.float32
BF16 = jnp.bfloat16


def sigmoid(v):
    return 1.0 / (1.0 + jnp.exp(-v))


def hand_on(hid, ssm, conv, hid_to, ssm_to, conv_to, sems):
    wide = ssm.shape[2] // PIECES
    copies = [
        pltpu.make_async_copy(ssm.at[:, :, k * wide : k * wide + wide], ssm_to.at[:, :, k * wide : k * wide + wide], sems.at[k])
        for k in range(PIECES)
    ]
    copies.append(pltpu.make_async_copy(conv, conv_to, sems.at[PIECES]))
    copies.append(pltpu.make_async_copy(hid, hid_to, sems.at[PIECES + 1]))
    for copy in copies:
        copy.start()
    for copy in copies:
        copy.wait()


def kernel(
    n, steps, slots, rank, states,
    pages_ref, paged_ref, rows_ref, gain_ref, conv_w_ref, conv_b_ref, dgain_ref, dbias_ref, lograte_ref, skip_ref,
    xw_hbm, zw_hbm, proj_hbm, dw_hbm, ow_hbm, ssm_hbm, conv_hbm,
    hid_ref, ssm_out, conv_out,
    xw, zw, ow, pw, dw,
    gath, accx, accz, ssq, state_in, state_fin, conv_in, conv_fin, win, act, delta, ysum,
    pf, part, part_in, red_out, proj_all, proj_f, mats, gated,
    send_a, recv_a, send_b, recv_b, send_c, recv_c,
    xw_sem, zw_sem, ow_sem, misc_sem,
    g_recv, g_s1, g_s2, g_s3,
    st_recv, st_send, cv_recv, cv_send,
    p_recv, p_send, q_recv, q_send,
    a_recv, a_send, b_recv, b_send, c_recv, c_send,
    so_recv, so_send, co_recv, co_send,
):
    me = lax.axis_index("tensor")
    bits = n.bit_length() - 1
    flips = [(1 - 2 * lax.rem(lax.div(me, 1 << k), 2)) * (1 << k) for k in range(bits)]

    def peer_of(j):
        out = me
        for k in range(bits):
            if isinstance(j, int):
                out = out + flips[k] if j >> k & 1 else out
            else:
                out = out + lax.rem(lax.div(j, 1 << k), 2) * flips[k]
        return out

    rows = rows_ref.shape[0]
    per = rows // steps
    dl = rows_ref.shape[1]
    cl = accx.shape[1]
    d_model = n * dl
    q = n // 4

    def order(i):
        if isinstance(i, int):
            return (i % (n // 2)) // 2 * 4 + i // (n // 2) * 2 + i % 2
        return lax.div(lax.rem(i, n // 2), 2) * 4 + lax.div(i, n // 2) * 2 + lax.rem(i, 2)

    def out_order(i):
        if isinstance(i, int):
            return 2 * i + 1 if i < n // 2 else 4 * (i - n // 2) + 2 if i < n // 2 + q else (4 * (i - n // 2 - q) + 4) % n
        return jnp.where(
            i < n // 2, 2 * i + 1,
            jnp.where(i < n // 2 + q, 4 * (i - n // 2) + 2, lax.rem(4 * jnp.maximum(i - n // 2 - q, 0) + 4, n)),
        )

    def cols(owner, width):
        return pl.ds(pl.multiple_of(owner * width, width), width)

    def x_load(i):
        src = xw_hbm.at[cols(peer_of(order(i)), dl), :]
        return pltpu.make_async_copy(src, xw.at[i], xw_sem.at[i])

    def z_load(i):
        src = zw_hbm.at[cols(peer_of(order(i)), dl), :]
        return pltpu.make_async_copy(src, zw.at[i], zw_sem.at[i])

    def o_load(i):
        if dl % LANES == 0:
            src = ow_hbm.at[:, cols(peer_of(out_order(i)), dl)]
        else:
            src = ow_hbm.at[peer_of(out_order(i))]
        return pltpu.make_async_copy(src, ow.at[i], ow_sem.at[i])

    p_load = pltpu.make_async_copy(proj_hbm, pw, misc_sem.at[0])
    d_load = pltpu.make_async_copy(dw_hbm, dw, misc_sem.at[1])
    own_state = pltpu.make_async_copy(ssm_hbm.at[:, :, cols(me, cl)], state_in.at[me], misc_sem.at[2])
    own_conv = pltpu.make_async_copy(conv_hbm.at[:, :, cols(me, cl)], conv_in.at[me], misc_sem.at[3])

    def remote(src, dst, ssem, rsem, peer):
        return pltpu.make_async_remote_copy(
            src_ref=src, dst_ref=dst, send_sem=ssem, recv_sem=rsem,
            device_id={"tensor": peer}, device_id_type=pl.DeviceIdType.MESH,
        )

    def to_core(j):
        return remote(gath.at[j], gath.at[j + 1], g_s1.at[j // 2 if isinstance(j, int) else lax.div(j, 2)], g_recv.at[j + 1], peer_of(1))

    def to_side(j):
        return remote(gath.at[j], gath.at[j + 2], g_s2.at[j // 4 if isinstance(j, int) else lax.div(j, 4)], g_recv.at[j + 2], peer_of(2))

    def to_far(k):
        return remote(gath.at[0], gath.at[4 * k], g_s3.at[k], g_recv.at[4 * k], peer_of(4 * k))

    def got(j):
        return remote(gath.at[0], gath.at[j], g_s3.at[0], g_recv.at[j], peer_of(1)).wait_recv()

    def state_copy(j, at):
        return remote(ssm_hbm.at[:, :, cols(peer_of(j), cl)], state_in.at[at], st_send.at[j], st_recv.at[j], peer_of(j))

    def conv_copy(j, at):
        return remote(conv_hbm.at[:, :, cols(peer_of(j), cl)], conv_in.at[at], cv_send.at[j], cv_recv.at[j], peer_of(j))

    def loop(lo, hi, flat=True):
        def wrap(f):
            if flat and hi - lo <= 16:
                for i in range(lo, hi):
                    f(i)
            else:
                lax.fori_loop(lo, hi, lambda i, c: (f(i), c)[1], 0)
        return wrap

    @loop(0, min(4, n))
    def _(i):
        x_load(i).start()
        z_load(i).start()

    barrier = pltpu.get_barrier_semaphore()

    @loop(1, n)
    def _(j):
        pl.semaphore_signal(barrier, inc=1, device_id={"tensor": peer_of(j)}, device_id_type=pl.DeviceIdType.MESH)

    page_row = paged_ref[0:1, :] * slots + paged_ref[1:2, :]
    spread = (lax.broadcasted_iota(jnp.int32, (per, per), 0) == page_row).astype(F32).astype(BF16)
    for t in range(steps):
        here = jnp.dot(spread, rows_ref[pl.ds(t * per, per), :], preferred_element_type=F32)
        gath[0, pl.ds(t * per, per), :] = here.astype(BF16)

    @loop(min(4, n), n)
    def _(i):
        x_load(i).start()
        z_load(i).start()

    p_load.start()
    d_load.start()
    own_state.start()
    own_conv.start()
    pl.semaphore_wait(barrier, n - 1)

    @loop(1, q)
    def _(k):
        to_far(k).start()

    to_side(0).start()
    to_core(0).start()

    accx[...] = jnp.zeros_like(accx)
    accz[...] = jnp.zeros_like(accz)
    ssq[...] = jnp.zeros_like(ssq)
    pf[...] = jnp.zeros_like(pf)

    @loop(0, n, False)
    def _(i):
        @pl.when(i < n // 2)
        def _():
            @pl.when(i >= 1)
            def _():
                conv_copy(2 * i, me).start()
                state_copy(2 * i, me).start()

            conv_copy(2 * i + 1, me).start()
            state_copy(2 * i + 1, me).start()

        @pl.when(i >= n // 2)
        def _():
            o_load(2 * i - n).start()
            o_load(2 * i - n + 1).start()

        @pl.when((lax.rem(i, 2) == 0) & (i + 2 < n))
        def _():
            j = order(i + 2)
            got(j)
            to_core(j).start()

            @pl.when(lax.rem(j, 4) == 0)
            def _():
                to_side(j).start()

        j = order(i)

        @pl.when(lax.rem(i, 2) == 1)
        def _():
            got(j)

        e = gath[j].astype(F32)
        ssq[...] += jnp.sum(e * e, axis=1, keepdims=True)
        a = (e * gain_ref[peer_of(j)]).astype(BF16)
        x_load(i).wait()
        accx[...] += jnp.dot(a, xw[i], preferred_element_type=F32)
        z_load(i).wait()
        accz[...] += jnp.dot(a, zw[i], preferred_element_type=F32)

    own_conv.wait()

    @loop(1, n)
    def _(j):
        conv_copy(j, peer_of(j)).wait_recv()

    @loop(0, n, False)
    def _(r):
        for s in range(slots):
            w = conv_in[r, s].astype(F32)
            for k in range(w.shape[0]):
                win[pl.ds(k * per + r * slots + s, 1), :] = w[k : k + 1]

    scale = lax.rsqrt(ssq[...] / d_model + 1e-06)
    taps = conv_w_ref.shape[0]
    win[pl.ds((taps - 1) * per, rows), :] = (accx[...] * scale).astype(BF16).astype(F32)
    zv = accz[...] * scale
    accz[...] = zv * sigmoid(zv)
    for t in range(steps):
        pre = conv_b_ref[...]
        for k in range(taps):
            pre = pre + win[pl.ds((t + k) * per, per), :] * conv_w_ref[k : k + 1]
        act[pl.ds(t * per, per), :] = pre * sigmoid(pre)

    p_load.wait()
    width = proj_hbm.shape[0]
    pf[:, :width] = lax.dot_general(
        act[...].astype(BF16), pw[...], (((1,), (1,)), ((), ())), preferred_element_type=F32
    )
    blocks = pf.shape[1] // LANES
    tiles = part.shape[1]
    used = rows // 16 * blocks
    for k in range(used, n * tiles):
        part[k // tiles, k % tiles] = jnp.zeros((16, LANES), SUM_TYPE)
    for k in range(used):
        g, b = divmod(k, blocks)
        part[k // tiles, k % tiles] = pf[16 * g : 16 * g + 16, LANES * b : LANES * b + LANES].astype(SUM_TYPE)

    def sum_copy(j):
        return remote(part.at[peer_of(j)], part_in.at[j], p_send.at[j], p_recv.at[j], peer_of(j))

    def share_copy(j, at):
        return remote(red_out, proj_all.at[at], q_send.at[j], q_recv.at[j], peer_of(j))

    @loop(1, n)
    def _(j):
        sum_copy(n - j).start()

    part_in[0] = part[me]

    @loop(1, n)
    def _(j):
        sum_copy(j).wait_recv()

    red = jnp.sum(part_in[...].astype(F32), axis=0).astype(SUM_TYPE)
    red_out[...] = red
    proj_all[me] = red

    @loop(1, n)
    def _(j):
        share_copy(n - j, me).start()

    @loop(1, n)
    def _(j):
        share_copy(j, peer_of(j)).wait_recv()

    for k in range(used):
        g, b = divmod(k, blocks)
        proj_f[16 * g : 16 * g + 16, LANES * b : LANES * b + LANES] = proj_all[k // tiles, k % tiles].astype(F32)

    low = proj_f[:, :rank]
    mats[...] = proj_f[:, rank : rank + LANES]
    norm = (low * lax.rsqrt(jnp.mean(low * low, axis=1, keepdims=True) + 1e-06) * dgain_ref[...]).astype(BF16)
    d_load.wait()
    pre = jnp.dot(norm, dw[...], preferred_element_type=F32) + dbias_ref[...]
    delta[...] = jnp.maximum(pre, 0.0) + jnp.log1p(jnp.exp(-jnp.abs(pre)))

    own_state.wait()
    rates = -jnp.exp(lograte_ref[...])

    def state_back(j, at):
        return remote(state_fin.at[peer_of(j)], ssm_out.at[:, :, cols(at, cl)], so_send.at[j], so_recv.at[j], peer_of(j))

    def conv_back(j, at):
        return remote(conv_fin.at[peer_of(j)], conv_out.at[:, :, cols(at, cl)], co_send.at[j], co_recv.at[j], peer_of(j))

    own_state_back = pltpu.make_async_copy(state_fin.at[me], ssm_out.at[:, :, cols(me, cl)], misc_sem.at[2])
    own_conv_back = pltpu.make_async_copy(conv_fin.at[me], conv_out.at[:, :, cols(me, cl)], misc_sem.at[3])
    lane = lax.broadcasted_iota(jnp.int32, (2 * states, LANES), 1)
    diag = lane == lax.broadcasted_iota(jnp.int32, (2 * states, LANES), 0)

    @loop(0, n, False)
    def _(i):
        j = n - 1 - i
        owner = peer_of(j)

        @pl.when(j > 0)
        def _():
            state_copy(j, owner).wait_recv()

        for s in range(slots):
            r = owner * slots + s
            h = state_in[owner, s].astype(F32)
            kept = []
            for t in range(steps):
                at = pl.ds(t * per + r, 1)
                both = jnp.sum(jnp.where(diag, mats[at, :], 0.0), axis=1, keepdims=True)
                dt = delta[at, :]
                h = h * jnp.exp(dt * rates) + (dt * act[at, :]) * both[:states]
                ysum[at, :] = jnp.sum(h * both[states:], axis=0, keepdims=True)
            state_fin[owner, s] = h.astype(BF16)
            kept = [win[pl.ds((steps + k) * per + r, 1), :] for k in range(taps - 1)]
            conv_fin[owner, s] = jnp.concatenate(kept, axis=0).astype(BF16)

        @pl.when(j > 0)
        def _():
            state_back(j, me).start()
            conv_back(j, me).start()

    own_state_back.start()
    own_conv_back.start()
    gated[...] = ((ysum[...] + skip_ref[...] * act[...]) * accz[...]).astype(BF16)

    def a_copy(k):
        return remote(send_a.at[k], recv_a.at[k], a_send.at[k], a_recv.at[k], peer_of(1))

    def b_copy(k):
        return remote(send_b.at[k], recv_b.at[k], b_send.at[k], b_recv.at[k], peer_of(2))

    def c_copy(k):
        return remote(send_c.at[k], recv_c.at[k], c_send.at[k], c_recv.at[k], peer_of(4 * k))

    def product(i):
        o_load(i).wait()
        return jnp.dot(gated[...], ow[i], preferred_element_type=F32)

    @loop(0, n // 2, False)
    def _(i):
        send_a[i] = product(i).astype(BF16)
        a_copy(i).start()

    @loop(0, q, False)
    def _(k):
        total = product(n // 2 + k)
        a_copy(2 * k + 1).wait_recv()
        send_b[k] = (total + recv_a[2 * k + 1].astype(F32)).astype(BF16)
        b_copy(k).start()

    @loop(1, q, False)
    def _(k):
        total = product(n // 2 + q + k - 1)
        a_copy(2 * k).wait_recv()
        b_copy(k).wait_recv()
        send_c[k] = (total + recv_a[2 * k].astype(F32) + recv_b[k].astype(F32)).astype(BF16)
        c_copy(k).start()

    total = product(n - 1) + gath[0].astype(F32)
    a_copy(0).wait_recv()
    b_copy(0).wait_recv()
    accum = total + recv_a[0].astype(F32) + recv_b[0].astype(F32)
    recv_c[0] = jnp.zeros((rows, dl), BF16)

    @loop(1, q)
    def _(k):
        c_copy(k).wait_recv()

    out = (accum + jnp.sum(recv_c[...].astype(F32), axis=0)).astype(BF16)
    page_col = pages_ref[:, 0:1] * slots + pages_ref[:, 1:2]
    pick = (lax.broadcasted_iota(jnp.int32, (per, per), 1) == page_col).astype(F32).astype(BF16)
    for t in range(steps):
        there = jnp.dot(pick, out[t * per : t * per + per], preferred_element_type=F32)
        hid_ref[pl.ds(t * per, per), :] = there.astype(BF16)

    own_state_back.wait()
    own_conv_back.wait()

    @loop(1, n)
    def _(j):
        state_back(j, peer_of(j)).wait_recv()
        conv_back(j, peer_of(j)).wait_recv()
        state_back(j, me).wait_send()
        conv_back(j, me).wait_send()
        state_copy(j, me).wait_send()
        conv_copy(j, me).wait_send()
        sum_copy(j).wait_send()
        share_copy(j, me).wait_send()

    @loop(1, q)
    def _(k):
        to_far(k).wait_send()
        c_copy(k).wait_send()

    @loop(0, q)
    def _(k):
        to_side(4 * k).wait_send()
        b_copy(k).wait_send()

    @loop(0, n // 2)
    def _(k):
        to_core(2 * k).wait_send()
        a_copy(k).wait_send()


def body(
    n, tokens, page_table, embedding, norm_gain, x_weight, z_weight, conv_weight, conv_bias, proj_weight,
    delta_gain, delta_weight, delta_bias, log_rates, skip_gain, out_weight, ssm_pages, conv_pages,
):
    steps, per = tokens.shape
    slots, states, _ = ssm_pages.shape
    window = conv_pages.shape[1]
    rank, cl = delta_weight.shape
    dl = embedding.shape[1]
    rows = steps * per
    q = n // 4
    local_rows = embedding[tokens.reshape(-1)]
    width = proj_weight.shape[1]
    blocks = -(-width // LANES)
    tiles = -(-(rows // 16 * blocks) // n)
    if dl % LANES == 0:
        out_w = out_weight
    else:
        out_w = out_weight.reshape(cl, n, dl).transpose(1, 0, 2)
    vm = pl.BlockSpec(memory_space=pltpu.VMEM)
    hbm = pl.BlockSpec(memory_space=pl.ANY)
    dma = pltpu.SemaphoreType.DMA
    V = pltpu.VMEM
    hid, ssm_out, conv_out = pl.pallas_call(
        functools.partial(kernel, n, steps, slots, rank, states),
        out_shape=(
            jax.ShapeDtypeStruct((rows, dl), BF16),
            jax.ShapeDtypeStruct(ssm_pages.shape, BF16),
            jax.ShapeDtypeStruct(conv_pages.shape, BF16),
        ),
        in_specs=[vm] * 10 + [hbm] * 7,
        out_specs=(vm, hbm, hbm),
        scratch_shapes=[
            V((n, dl, cl), BF16), V((n, dl, cl), BF16), V((n, cl, dl), BF16), V((width, cl), BF16), V((rank, cl), BF16),
            V((n, rows, dl), BF16), V((rows, cl), F32), V((rows, cl), F32), V((rows, 1), F32),
            V((n, slots, states, cl), BF16), V((n, slots, states, cl), BF16),
            V((n, slots, window, cl), BF16), V((n, slots, window, cl), BF16),
            V((window * per + rows, cl), F32), V((rows, cl), F32), V((rows, cl), F32), V((rows, cl), F32),
            V((rows, blocks * LANES), F32), V((n, tiles, 16, LANES), SUM_TYPE), V((n, tiles, 16, LANES), SUM_TYPE),
            V((tiles, 16, LANES), SUM_TYPE), V((n, tiles, 16, LANES), SUM_TYPE), V((rows, blocks * LANES), F32), V((rows, LANES), F32), V((rows, cl), BF16),
            V((n // 2, rows, dl), BF16), V((n // 2, rows, dl), BF16),
            V((q, rows, dl), BF16), V((q, rows, dl), BF16), V((q, rows, dl), BF16), V((q, rows, dl), BF16),
            dma((n,)), dma((n,)), dma((n,)), dma((4,)),
            dma((n,)), dma((n // 2,)), dma((q,)), dma((q,)),
        ] + [dma((n,))] * 8 + [
            dma((n // 2,)), dma((n // 2,)), dma((q,)), dma((q,)), dma((q,)), dma((q,)),
        ] + [dma((n,))] * 4,
        compiler_params=pltpu.CompilerParams(
            collective_id=0, has_side_effects=True, vmem_limit_bytes=62 * 1024 * 1024
        ),
        cost_estimate=pl.CostEstimate(flops=2 * rows * cl * dl * n * 3, bytes_accessed=6 * cl * dl * n, transcendentals=0),
    )(
        page_table, page_table.T, local_rows, norm_gain.reshape(n, 1, dl), conv_weight, conv_bias.reshape(1, cl), delta_gain.reshape(1, rank),
        delta_bias.reshape(1, cl), log_rates, skip_gain.reshape(1, cl),
        x_weight, z_weight, proj_weight.T, delta_weight, out_w, ssm_pages, conv_pages,
    )
    hid, ssm_out, conv_out = pl.pallas_call(
        hand_on,
        out_shape=tuple(jax.ShapeDtypeStruct(v.shape, v.dtype) for v in (hid, ssm_out, conv_out)),
        in_specs=[hbm] * 3,
        out_specs=(hbm,) * 3,
        scratch_shapes=[dma((PIECES + 2,))],
    )(hid, ssm_out, conv_out)
    return hid.reshape(steps, per, dl), ssm_out, conv_out


def solution(mesh):
    placed = (
        P(None, "groups"),
        P("groups", None),
        P(None, "tensor"),
        P(),
        P(None, "tensor"),
        P(None, "tensor"),
        P(None, "tensor"),
        P("tensor"),
        P("tensor", None),
        P(),
        P(None, "tensor"),
        P("tensor"),
        P(None, "tensor"),
        P("tensor"),
        P("tensor", None),
        P(("groups", "tensor"), None, None),
        P(("groups", "tensor"), None, None),
    )
    return jax.shard_map(
        functools.partial(body, mesh.shape["tensor"]),
        mesh=mesh,
        in_specs=placed,
        out_specs=(
            P(None, "groups", "tensor"),
            P(("groups", "tensor"), None, None),
            P(("groups", "tensor"), None, None),
        ),
        check_vma=False,
    )
```

```python
import functools

import jax
import jax.numpy as jnp
from jax import lax
from jax.experimental import pallas as pl
from jax.experimental.pallas import tpu as pltpu
from jax.sharding import PartitionSpec as P

LANES = 128
PIECES = 4
SUM_TYPE = jnp.float32
F32 = jnp.float32
BF16 = jnp.bfloat16


def sigmoid(v):
    return 1.0 / (1.0 + jnp.exp(-v))


def hand_on(hid, ssm, conv, hid_to, ssm_to, conv_to, hid_v, ssm_v, conv_v, sems):
    wide = ssm.shape[2] // PIECES
    hops = [
        (ssm.at[:, :, k * wide : k * wide + wide], ssm_v.at[k], ssm_to.at[:, :, k * wide : k * wide + wide])
        for k in range(PIECES)
    ]
    hops += [(conv, conv_v, conv_to), (hid, hid_v, hid_to)]
    into = [pltpu.make_async_copy(a, b, sems.at[0, k]) for k, (a, b, _) in enumerate(hops)]
    away = [pltpu.make_async_copy(b, c, sems.at[1, k]) for k, (_, b, c) in enumerate(hops)]
    for copy in into:
        copy.start()
    for first, second in zip(into, away):
        first.wait()
        second.start()
    for copy in away:
        copy.wait()


def kernel(
    n, steps, slots, rank, states,
    paged_ref, rows_ref, gain_ref, conv_w_ref, conv_b_ref, dgain_ref, dbias_ref, lograte_ref, skip_ref,
    xw_hbm, zw_hbm, proj_hbm, dw_hbm, ow_hbm, ssm_hbm, conv_hbm,
    hid_ref, ssm_out, conv_out,
    xw, zw, ow, pw, dw,
    gath, accx, accz, ssq, state_in, state_fin, conv_in, conv_fin, win, act, delta, ysum,
    pf, part, part_in, red_out, proj_all, proj_f, mats, gated,
    send_a, recv_a, send_b, recv_b, send_c, recv_c,
    xw_sem, zw_sem, ow_sem, misc_sem,
    g_recv, g_s1, g_s2, g_s3,
    st_recv, st_send, cv_recv, cv_send,
    p_recv, p_send, q_recv, q_send,
    a_recv, a_send, b_recv, b_send, c_recv, c_send,
    so_recv, so_send, co_recv, co_send,
):
    me = lax.axis_index("tensor")
    bits = n.bit_length() - 1
    flips = [(1 - 2 * lax.rem(lax.div(me, 1 << k), 2)) * (1 << k) for k in range(bits)]

    def peer_of(j):
        out = me
        for k in range(bits):
            if isinstance(j, int):
                out = out + flips[k] if j >> k & 1 else out
            else:
                out = out + lax.rem(lax.div(j, 1 << k), 2) * flips[k]
        return out

    rows = rows_ref.shape[0]
    per = rows // steps
    dl = rows_ref.shape[1]
    cl = accx.shape[1]
    d_model = n * dl
    q = n // 4

    def order(i):
        if isinstance(i, int):
            return (i % (n // 2)) // 2 * 4 + i // (n // 2) * 2 + i % 2
        return lax.div(lax.rem(i, n // 2), 2) * 4 + lax.div(i, n // 2) * 2 + lax.rem(i, 2)

    def out_order(i):
        if isinstance(i, int):
            return 2 * i + 1 if i < n // 2 else 4 * (i - n // 2) + 2 if i < n // 2 + q else (4 * (i - n // 2 - q) + 4) % n
        return jnp.where(
            i < n // 2, 2 * i + 1,
            jnp.where(i < n // 2 + q, 4 * (i - n // 2) + 2, lax.rem(4 * jnp.maximum(i - n // 2 - q, 0) + 4, n)),
        )

    def cols(owner, width):
        return pl.ds(pl.multiple_of(owner * width, width), width)

    def x_load(i):
        src = xw_hbm.at[cols(peer_of(order(i)), dl), :]
        return pltpu.make_async_copy(src, xw.at[i], xw_sem.at[i])

    def z_load(i):
        src = zw_hbm.at[cols(peer_of(order(i)), dl), :]
        return pltpu.make_async_copy(src, zw.at[i], zw_sem.at[i])

    def o_load(i):
        if dl % LANES == 0:
            src = ow_hbm.at[:, cols(peer_of(out_order(i)), dl)]
        else:
            src = ow_hbm.at[peer_of(out_order(i))]
        return pltpu.make_async_copy(src, ow.at[i], ow_sem.at[i])

    p_load = pltpu.make_async_copy(proj_hbm, pw, misc_sem.at[0])
    d_load = pltpu.make_async_copy(dw_hbm, dw, misc_sem.at[1])
    own_state = pltpu.make_async_copy(ssm_hbm.at[:, :, cols(me, cl)], state_in.at[me], misc_sem.at[2])
    own_conv = pltpu.make_async_copy(conv_hbm.at[:, :, cols(me, cl)], conv_in.at[me], misc_sem.at[3])

    def remote(src, dst, ssem, rsem, peer):
        return pltpu.make_async_remote_copy(
            src_ref=src, dst_ref=dst, send_sem=ssem, recv_sem=rsem,
            device_id={"tensor": peer}, device_id_type=pl.DeviceIdType.MESH,
        )

    def to_core(j):
        return remote(gath.at[j], gath.at[j + 1], g_s1.at[j // 2 if isinstance(j, int) else lax.div(j, 2)], g_recv.at[j + 1], peer_of(1))

    def to_side(j):
        return remote(gath.at[j], gath.at[j + 2], g_s2.at[j // 4 if isinstance(j, int) else lax.div(j, 4)], g_recv.at[j + 2], peer_of(2))

    def to_far(k):
        return remote(gath.at[0], gath.at[4 * k], g_s3.at[k], g_recv.at[4 * k], peer_of(4 * k))

    def got(j):
        return remote(gath.at[0], gath.at[j], g_s3.at[0], g_recv.at[j], peer_of(1)).wait_recv()

    def state_copy(j, at):
        return remote(ssm_hbm.at[:, :, cols(peer_of(j), cl)], state_in.at[at], st_send.at[j], st_recv.at[j], peer_of(j))

    def conv_copy(j, at):
        return remote(conv_hbm.at[:, :, cols(peer_of(j), cl)], conv_in.at[at], cv_send.at[j], cv_recv.at[j], peer_of(j))

    def loop(lo, hi, flat=True):
        def wrap(f):
            if flat and hi - lo <= 16:
                for i in range(lo, hi):
                    f(i)
            else:
                lax.fori_loop(lo, hi, lambda i, c: (f(i), c)[1], 0)
        return wrap

    @loop(0, min(4, n))
    def _(i):
        x_load(i).start()
        z_load(i).start()

    barrier = pltpu.get_barrier_semaphore()

    @loop(1, n)
    def _(j):
        pl.semaphore_signal(barrier, inc=1, device_id={"tensor": peer_of(j)}, device_id_type=pl.DeviceIdType.MESH)

    page_row = paged_ref[0:1, :] * slots + paged_ref[1:2, :]
    spread = (lax.broadcasted_iota(jnp.int32, (per, per), 0) == page_row).astype(F32).astype(BF16)
    for t in range(steps):
        here = jnp.dot(spread, rows_ref[pl.ds(t * per, per), :], preferred_element_type=F32)
        gath[0, pl.ds(t * per, per), :] = here.astype(BF16)

    @loop(min(4, n), n)
    def _(i):
        x_load(i).start()
        z_load(i).start()

    p_load.start()
    d_load.start()
    own_state.start()
    own_conv.start()
    pl.semaphore_wait(barrier, n - 1)

    @loop(1, q)
    def _(k):
        to_far(k).start()

    to_side(0).start()
    to_core(0).start()

    accx[...] = jnp.zeros_like(accx)
    accz[...] = jnp.zeros_like(accz)
    ssq[...] = jnp.zeros_like(ssq)
    pf[...] = jnp.zeros_like(pf)

    @loop(0, n, False)
    def _(i):
        @pl.when(i < n // 2)
        def _():
            @pl.when(i >= 1)
            def _():
                conv_copy(2 * i, me).start()
                state_copy(2 * i, me).start()

            conv_copy(2 * i + 1, me).start()
            state_copy(2 * i + 1, me).start()

        @pl.when(i >= n // 2)
        def _():
            o_load(2 * i - n).start()
            o_load(2 * i - n + 1).start()

        @pl.when((lax.rem(i, 2) == 0) & (i + 2 < n))
        def _():
            j = order(i + 2)
            got(j)
            to_core(j).start()

            @pl.when(lax.rem(j, 4) == 0)
            def _():
                to_side(j).start()

        j = order(i)

        @pl.when(lax.rem(i, 2) == 1)
        def _():
            got(j)

        e = gath[j].astype(F32)
        ssq[...] += jnp.sum(e * e, axis=1, keepdims=True)
        a = (e * gain_ref[peer_of(j)]).astype(BF16)
        x_load(i).wait()
        accx[...] += jnp.dot(a, xw[i], preferred_element_type=F32)
        z_load(i).wait()
        accz[...] += jnp.dot(a, zw[i], preferred_element_type=F32)

    own_conv.wait()

    @loop(1, n)
    def _(j):
        conv_copy(j, peer_of(j)).wait_recv()

    @loop(0, n, False)
    def _(r):
        for s in range(slots):
            w = conv_in[r, s].astype(F32)
            for k in range(w.shape[0]):
                win[pl.ds(k * per + r * slots + s, 1), :] = w[k : k + 1]

    scale = lax.rsqrt(ssq[...] / d_model + 1e-06)
    taps = conv_w_ref.shape[0]
    win[pl.ds((taps - 1) * per, rows), :] = (accx[...] * scale).astype(BF16).astype(F32)
    zv = accz[...] * scale
    accz[...] = zv * sigmoid(zv)
    for t in range(steps):
        pre = conv_b_ref[...]
        for k in range(taps):
            pre = pre + win[pl.ds((t + k) * per, per), :] * conv_w_ref[k : k + 1]
        act[pl.ds(t * per, per), :] = pre * sigmoid(pre)

    p_load.wait()
    width = proj_hbm.shape[0]
    pf[:, :width] = lax.dot_general(
        act[...].astype(BF16), pw[...], (((1,), (1,)), ((), ())), preferred_element_type=F32
    )
    blocks = pf.shape[1] // LANES
    tiles = part.shape[1]
    used = rows // 16 * blocks
    for k in range(used, n * tiles):
        part[k // tiles, k % tiles] = jnp.zeros((16, LANES), SUM_TYPE)
    for k in range(used):
        g, b = divmod(k, blocks)
        part[k // tiles, k % tiles] = pf[16 * g : 16 * g + 16, LANES * b : LANES * b + LANES].astype(SUM_TYPE)

    def sum_copy(j):
        return remote(part.at[peer_of(j)], part_in.at[j], p_send.at[j], p_recv.at[j], peer_of(j))

    def share_copy(j, at):
        return remote(red_out, proj_all.at[at], q_send.at[j], q_recv.at[j], peer_of(j))

    @loop(1, n)
    def _(j):
        sum_copy(n - j).start()

    part_in[0] = part[me]

    @loop(1, n)
    def _(j):
        sum_copy(j).wait_recv()

    red = jnp.sum(part_in[...].astype(F32), axis=0).astype(SUM_TYPE)
    red_out[...] = red
    proj_all[me] = red

    @loop(1, n)
    def _(j):
        share_copy(n - j, me).start()

    @loop(1, n)
    def _(j):
        share_copy(j, peer_of(j)).wait_recv()

    for k in range(used):
        g, b = divmod(k, blocks)
        proj_f[16 * g : 16 * g + 16, LANES * b : LANES * b + LANES] = proj_all[k // tiles, k % tiles].astype(F32)

    low = proj_f[:, :rank]
    mats[...] = proj_f[:, rank : rank + LANES]
    norm = (low * lax.rsqrt(jnp.mean(low * low, axis=1, keepdims=True) + 1e-06) * dgain_ref[...]).astype(BF16)
    d_load.wait()
    pre = jnp.dot(norm, dw[...], preferred_element_type=F32) + dbias_ref[...]
    delta[...] = jnp.maximum(pre, 0.0) + jnp.log1p(jnp.exp(-jnp.abs(pre)))

    own_state.wait()
    rates = -jnp.exp(lograte_ref[...])

    def state_back(j, at):
        return remote(state_fin.at[peer_of(j)], ssm_out.at[:, :, cols(at, cl)], so_send.at[j], so_recv.at[j], peer_of(j))

    def conv_back(j, at):
        return remote(conv_fin.at[peer_of(j)], conv_out.at[:, :, cols(at, cl)], co_send.at[j], co_recv.at[j], peer_of(j))

    own_state_back = pltpu.make_async_copy(state_fin.at[me], ssm_out.at[:, :, cols(me, cl)], misc_sem.at[2])
    own_conv_back = pltpu.make_async_copy(conv_fin.at[me], conv_out.at[:, :, cols(me, cl)], misc_sem.at[3])
    lane = lax.broadcasted_iota(jnp.int32, (2 * states, LANES), 1)
    diag = lane == lax.broadcasted_iota(jnp.int32, (2 * states, LANES), 0)

    @loop(0, n, False)
    def _(i):
        j = n - 1 - i
        owner = peer_of(j)

        @pl.when(j > 0)
        def _():
            state_copy(j, owner).wait_recv()

        for s in range(slots):
            r = owner * slots + s
            h = state_in[owner, s].astype(F32)
            kept = []
            for t in range(steps):
                at = pl.ds(t * per + r, 1)
                both = jnp.sum(jnp.where(diag, mats[at, :], 0.0), axis=1, keepdims=True)
                dt = delta[at, :]
                h = h * jnp.exp(dt * rates) + (dt * act[at, :]) * both[:states]
                ysum[at, :] = jnp.sum(h * both[states:], axis=0, keepdims=True)
            state_fin[owner, s] = h.astype(BF16)
            kept = [win[pl.ds((steps + k) * per + r, 1), :] for k in range(taps - 1)]
            conv_fin[owner, s] = jnp.concatenate(kept, axis=0).astype(BF16)

        @pl.when(j > 0)
        def _():
            state_back(j, me).start()
            conv_back(j, me).start()

    own_state_back.start()
    own_conv_back.start()
    gated[...] = ((ysum[...] + skip_ref[...] * act[...]) * accz[...]).astype(BF16)

    def a_copy(k):
        return remote(send_a.at[k], recv_a.at[k], a_send.at[k], a_recv.at[k], peer_of(1))

    def b_copy(k):
        return remote(send_b.at[k], recv_b.at[k], b_send.at[k], b_recv.at[k], peer_of(2))

    def c_copy(k):
        return remote(send_c.at[k], recv_c.at[k], c_send.at[k], c_recv.at[k], peer_of(4 * k))

    def product(i):
        o_load(i).wait()
        return jnp.dot(gated[...], ow[i], preferred_element_type=F32)

    @loop(0, n // 2, False)
    def _(i):
        send_a[i] = product(i).astype(BF16)
        a_copy(i).start()

    @loop(0, q, False)
    def _(k):
        total = product(n // 2 + k)
        a_copy(2 * k + 1).wait_recv()
        send_b[k] = (total + recv_a[2 * k + 1].astype(F32)).astype(BF16)
        b_copy(k).start()

    @loop(1, q, False)
    def _(k):
        total = product(n // 2 + q + k - 1)
        a_copy(2 * k).wait_recv()
        b_copy(k).wait_recv()
        send_c[k] = (total + recv_a[2 * k].astype(F32) + recv_b[k].astype(F32)).astype(BF16)
        c_copy(k).start()

    total = product(n - 1) + gath[0].astype(F32)
    a_copy(0).wait_recv()
    b_copy(0).wait_recv()
    accum = total + recv_a[0].astype(F32) + recv_b[0].astype(F32)
    recv_c[0] = jnp.zeros((rows, dl), BF16)

    @loop(1, q)
    def _(k):
        c_copy(k).wait_recv()

    out = (accum + jnp.sum(recv_c[...].astype(F32), axis=0)).astype(BF16)
    ids = jnp.broadcast_to((paged_ref[0:1, :] * slots + paged_ref[1:2, :]).astype(F32), (per, per))
    across = lax.broadcasted_iota(jnp.int32, (per, per), 1)
    down = lax.broadcasted_iota(jnp.int32, (per, per), 0)
    page_col = jnp.sum(jnp.where(across == down, ids, 0.0), axis=1, keepdims=True)
    pick = (across.astype(F32) == page_col).astype(F32).astype(BF16)
    for t in range(steps):
        there = jnp.dot(pick, out[t * per : t * per + per], preferred_element_type=F32)
        hid_ref[pl.ds(t * per, per), :] = there.astype(BF16)

    own_state_back.wait()
    own_conv_back.wait()

    @loop(1, n)
    def _(j):
        state_back(j, peer_of(j)).wait_recv()
        conv_back(j, peer_of(j)).wait_recv()
        state_back(j, me).wait_send()
        conv_back(j, me).wait_send()
        state_copy(j, me).wait_send()
        conv_copy(j, me).wait_send()
        sum_copy(j).wait_send()
        share_copy(j, me).wait_send()

    @loop(1, q)
    def _(k):
        to_far(k).wait_send()
        c_copy(k).wait_send()

    @loop(0, q)
    def _(k):
        to_side(4 * k).wait_send()
        b_copy(k).wait_send()

    @loop(0, n // 2)
    def _(k):
        to_core(2 * k).wait_send()
        a_copy(k).wait_send()


def body(
    n, tokens, page_table, embedding, norm_gain, x_weight, z_weight, conv_weight, conv_bias, proj_weight,
    delta_gain, delta_weight, delta_bias, log_rates, skip_gain, out_weight, ssm_pages, conv_pages,
):
    steps, per = tokens.shape
    slots, states, _ = ssm_pages.shape
    window = conv_pages.shape[1]
    rank, cl = delta_weight.shape
    dl = embedding.shape[1]
    rows = steps * per
    q = n // 4
    local_rows = embedding[tokens.reshape(-1)]
    width = proj_weight.shape[1]
    blocks = -(-width // LANES)
    tiles = -(-(rows // 16 * blocks) // n)
    if dl % LANES == 0:
        out_w = out_weight
    else:
        out_w = out_weight.reshape(cl, n, dl).transpose(1, 0, 2)
    vm = pl.BlockSpec(memory_space=pltpu.VMEM)
    hbm = pl.BlockSpec(memory_space=pl.ANY)
    dma = pltpu.SemaphoreType.DMA
    V = pltpu.VMEM
    hid, ssm_out, conv_out = pl.pallas_call(
        functools.partial(kernel, n, steps, slots, rank, states),
        out_shape=(
            jax.ShapeDtypeStruct((rows, dl), BF16),
            jax.ShapeDtypeStruct(ssm_pages.shape, BF16),
            jax.ShapeDtypeStruct(conv_pages.shape, BF16),
        ),
        in_specs=[vm] * 9 + [hbm] * 7,
        out_specs=(vm, hbm, hbm),
        scratch_shapes=[
            V((n, dl, cl), BF16), V((n, dl, cl), BF16), V((n, cl, dl), BF16), V((width, cl), BF16), V((rank, cl), BF16),
            V((n, rows, dl), BF16), V((rows, cl), F32), V((rows, cl), F32), V((rows, 1), F32),
            V((n, slots, states, cl), BF16), V((n, slots, states, cl), BF16),
            V((n, slots, window, cl), BF16), V((n, slots, window, cl), BF16),
            V((window * per + rows, cl), F32), V((rows, cl), F32), V((rows, cl), F32), V((rows, cl), F32),
            V((rows, blocks * LANES), F32), V((n, tiles, 16, LANES), SUM_TYPE), V((n, tiles, 16, LANES), SUM_TYPE),
            V((tiles, 16, LANES), SUM_TYPE), V((n, tiles, 16, LANES), SUM_TYPE), V((rows, blocks * LANES), F32), V((rows, LANES), F32), V((rows, cl), BF16),
            V((n // 2, rows, dl), BF16), V((n // 2, rows, dl), BF16),
            V((q, rows, dl), BF16), V((q, rows, dl), BF16), V((q, rows, dl), BF16), V((q, rows, dl), BF16),
            dma((n,)), dma((n,)), dma((n,)), dma((4,)),
            dma((n,)), dma((n // 2,)), dma((q,)), dma((q,)),
        ] + [dma((n,))] * 8 + [
            dma((n // 2,)), dma((n // 2,)), dma((q,)), dma((q,)), dma((q,)), dma((q,)),
        ] + [dma((n,))] * 4,
        compiler_params=pltpu.CompilerParams(
            collective_id=0, has_side_effects=True, vmem_limit_bytes=62 * 1024 * 1024
        ),
        cost_estimate=pl.CostEstimate(flops=2 * rows * cl * dl * n * 3, bytes_accessed=6 * cl * dl * n, transcendentals=0),
    )(
        page_table.T, local_rows, norm_gain.reshape(n, 1, dl), conv_weight, conv_bias.reshape(1, cl), delta_gain.reshape(1, rank),
        delta_bias.reshape(1, cl), log_rates, skip_gain.reshape(1, cl),
        x_weight, z_weight, proj_weight.T, delta_weight, out_w, ssm_pages, conv_pages,
    )
    hid, ssm_out, conv_out = pl.pallas_call(
        hand_on,
        out_shape=tuple(jax.ShapeDtypeStruct(v.shape, v.dtype) for v in (hid, ssm_out, conv_out)),
        in_specs=[hbm] * 3,
        out_specs=(hbm,) * 3,
        scratch_shapes=[
            V(hid.shape, BF16), V((PIECES, slots, states, ssm_out.shape[2] // PIECES), BF16), V(conv_out.shape, BF16),
            dma((2, PIECES + 2)),
        ],
    )(hid, ssm_out, conv_out)
    return hid.reshape(steps, per, dl), ssm_out, conv_out


def solution(mesh):
    placed = (
        P(None, "groups"),
        P("groups", None),
        P(None, "tensor"),
        P(),
        P(None, "tensor"),
        P(None, "tensor"),
        P(None, "tensor"),
        P("tensor"),
        P("tensor", None),
        P(),
        P(None, "tensor"),
        P("tensor"),
        P(None, "tensor"),
        P("tensor"),
        P("tensor", None),
        P(("groups", "tensor"), None, None),
        P(("groups", "tensor"), None, None),
    )
    return jax.shard_map(
        functools.partial(body, mesh.shape["tensor"]),
        mesh=mesh,
        in_specs=placed,
        out_specs=(
            P(None, "groups", "tensor"),
            P(("groups", "tensor"), None, None),
            P(("groups", "tensor"), None, None),
        ),
        check_vma=False,
    )
```
